32 devices in a mesh: groups: 2 (over x), fsdp: 16 (over z, y, core).
Axes of the slice: x: 2, y: 2, z: 4, core: 2. Of those that a mesh axis runs over, the one named last changes fastest.
Arguments:
- tokens: bfloat16 [4096, 8192], P(('groups', 'fsdp')), parts along dimension 0
- upstream: bfloat16 [4096, 1024], P(('groups', 'fsdp')), parts along dimension 0, may hold values from -3 to 3
- norm_gain: float32 [8192], replicated, may hold values from 0.25 to 1.75
- value_weight: bfloat16 [8192, 1024], P('fsdp'), may hold values from -0.0625 to 0.0625
- down_factor: bfloat16 [8192, 2048], P('fsdp'), may hold values from -0.0625 to 0.0625
- up_factor: bfloat16 [1024, 2048], P('fsdp'), may hold values from -0.75 to 0.75
- tenant: int32 [64], P('groups'), parts along dimension 0, may hold values from 0 to 31
Outputs:
- adapted_values: bfloat16 [4096, 1024], P(('groups', 'fsdp')), parts along dimension 0
- grad_tokens: bfloat16 [4096, 8192], P(('groups', 'fsdp')), parts along dimension 0
- grad_down: float32 [16384, 2048], P(('groups', 'fsdp')), parts along dimension 0
- grad_up: float32 [2048, 2048], P(('groups', 'fsdp')), parts along dimension 0
The draws below stay inside these ranges and needn't reach their ends.
There are 2 independent parts, one for each index of `groups`. The reference program is written for one: setup_inputs(seed, part) draws one part's arguments, and reference() takes and returns one part's arrays. A program takes and returns all parts, laid end to end along the dimension named above; an argument that names none is the same for every part. Nothing has to cross between parts.
Inputs may be any that keep to these rules, and one draw needn't show every extreme that they name: `tenant`: adapter ids, one for each block of 64 tokens.
All inputs are finite; a program needn't handle non-finite values.
Results may differ from the reference program's by a relative error of at most 0.0051.
Values may be sent and summed in bfloat16 or wider, within the bound.
No kernel may reach another device: no remote copies, remote signals or barrier semaphores. Data moves between devices by JAX's collectives and lax.ppermute only.
A program may use at most 128 MiB of HBM per device.

```python
import math
import jax
import jax.numpy as jnp
import numpy as np
from jax import lax

D = 8192
VALUE_HEAD_WIDTH = 1024
RANK = 64
BLK = 64
NBLOCKS = 32
TOKENS = 2048
ADAPTERS = 32


def draw_tokens(key, part):
    key = jax.random.fold_in(key, 11)
    key_noise, key_rows, key_columns = jax.random.split(key, 3)
    row_scale = jnp.exp(jax.random.uniform(key_rows, (TOKENS, 1), jnp.float32, jnp.log(0.3), jnp.log(3.0)))
    column_scale = jnp.exp(jax.random.uniform(key_columns, (1, D), jnp.float32, jnp.log(0.4), jnp.log(4.0)))
    noise = jax.random.normal(key_noise, (TOKENS, D), jnp.float32)
    return (noise * row_scale * column_scale).astype(jnp.bfloat16)


def touch_ends(entries, rng, smallest, largest):
    index_at = [jax.random.randint(jax.random.fold_in(rng, axis), (), 0, length) for axis, length in enumerate(entries.shape)]
    main_axis = entries.shape.index(max(entries.shape))
    neighbour = index_at[:main_axis] + [(index_at[main_axis] + 1) % entries.shape[main_axis]] + index_at[main_axis + 1:]
    return entries.at[tuple(index_at)].set(smallest).at[tuple(neighbour)].set(largest)


def strengthened(result, stream_key, source, target, shards_of, factor):
    def block_of(axis_at):
        return (jnp.arange(result.shape[axis_at]) // (result.shape[axis_at] // shards_of)).reshape((-1,) + (1,) * (result.ndim - 1 - axis_at))

    one_side = jax.random.permutation(stream_key, shards_of)[block_of(target)]
    second = (block_of(target) + shards_of // 2) % shards_of
    return jnp.where((block_of(source) == one_side) | (block_of(source) == second), factor * result, result)


def levels(key, shape, shards, least, largest):
    factor_of, own = 1.0, jax.random.fold_in(key, 6)
    for dim, shards_of in shards:
        heights = jnp.exp(jax.random.uniform(jax.random.fold_in(own, dim), (shards_of,), jnp.float32, least / len(shards), largest / len(shards)))
        factor_of = factor_of * jnp.repeat(heights, shape[dim] // shards_of).reshape([-1 if axis == dim else 1 for axis in range(len(shape))])
    return factor_of


def rank_table(count, skew):
    weights = [(1 << 20) // math.isqrt(rank ** skew) + 1 for rank in range(1, count + 1)]
    scale = 1 + sum(weights) // (1 << 30)
    return np.cumsum(np.array([max(1, weight // scale) for weight in weights]))


def skewed_ids(key, dims, number_of, slope):
    table = rank_table(number_of, slope)
    pick = jax.random.randint(jax.random.fold_in(key, 1), dims, 0, int(table[number_of - 1]))
    grade = jnp.searchsorted(jnp.asarray(table, jnp.int32), pick, side="right")
    return jax.random.permutation(jax.random.fold_in(key, 2), number_of)[grade].astype(jnp.int32)


def scatter_about(key, extent, spread, most, pieces=(), held_as=jnp.bfloat16):
    level = levels(key, extent, pieces, -0.22, 0.18) if pieces else 1.0
    entries = jax.random.normal(key, extent, jnp.float32) * spread * level
    return jnp.minimum(jnp.maximum(entries, -most), most).astype(held_as)


def bell_draw_with(own_key, shape, scale, limit, cuts, heavy, held_as=jnp.bfloat16):
    array = scale * jax.random.normal(own_key, shape, jnp.float32)
    if cuts:
        array = array * levels(own_key, shape, cuts, -0.22, 0.18)
    return jnp.clip(strengthened(array, jax.random.fold_in(own_key, 3), *heavy), -limit, limit).astype(held_as)


def setup_inputs(seed: int = 0, part: int = 0) -> dict:
    arg_keys = jax.random.split(jax.random.key(seed), 8)
    own_keys = jax.random.split(jax.random.fold_in(arg_keys[7], part), 8)
    return {
        "tokens": draw_tokens(jax.random.fold_in(jax.random.fold_in(arg_keys[7], part), 71), part),
        "upstream": bell_draw_with(own_keys[1], (TOKENS, VALUE_HEAD_WIDTH), 0.5, 3.0, ((0, 16),), (0, 1, 16, 2.0)),
        "norm_gain": jnp.clip(1.0 + 0.15 * jax.random.normal(arg_keys[2], (D,), jnp.float32), 0.25, 1.75),
        "value_weight": scatter_about(arg_keys[3], (D, VALUE_HEAD_WIDTH), D ** -0.5, 0.0625, ((0, 16),)),
        "down_factor": scatter_about(arg_keys[4], (D, ADAPTERS * RANK), D ** -0.5, 0.0625, ((0, 16),)),
        "up_factor": scatter_about(arg_keys[5], (VALUE_HEAD_WIDTH, ADAPTERS * RANK), RANK ** -0.5, 0.75, ((0, 16),)),
        "tenant": touch_ends(skewed_ids(own_keys[6], (NBLOCKS,), ADAPTERS, 2), jax.random.fold_in(own_keys[6], 3), 0, ADAPTERS - 1).astype(jnp.int32),
    }


adapter_scale = 0.5
norm_eps = 1e-05

def reference(tokens, upstream, norm_gain, value_weight, down_factor, up_factor, tenant):
    wide_tokens = tokens.astype(jnp.float32)
    inverse = lax.rsqrt(lax.optimization_barrier(jnp.mean(wide_tokens * wide_tokens, axis=1, keepdims=True)) + norm_eps)
    normed = (wide_tokens * inverse * norm_gain).astype(jnp.bfloat16)
    blocks = tenant.shape[0]
    normalized_blocks = normed.reshape(blocks, BLK, D)
    upstream_blocks = upstream.reshape(blocks, BLK, VALUE_HEAD_WIDTH)

    def block_step(carry, inputs):
        sum_down, sum_up = carry
        rows_normed, upstream_gradient_rows, which = inputs
        start = (which * RANK).astype(jnp.int32)
        down = lax.dynamic_slice_in_dim(down_factor, start, RANK, 1)
        up = lax.dynamic_slice_in_dim(up_factor, start, RANK, 1)
        low_rank_rows = jnp.dot(rows_normed, down, preferred_element_type=jnp.float32).astype(jnp.bfloat16)
        adapter_branch = lax.dot_general(low_rank_rows, up, (((1,), (1,)), ((), ())), preferred_element_type=jnp.float32)
        mixed_output = jnp.dot(upstream_gradient_rows, up, preferred_element_type=jnp.float32)
        scaled_update = (adapter_scale * mixed_output).astype(jnp.bfloat16)
        back_side = lax.dot_general(scaled_update, down, (((1,), (1,)), ((), ())), preferred_element_type=jnp.float32)
        term_down = lax.dot_general(rows_normed, scaled_update, (((0,), (0,)), ((), ())), preferred_element_type=jnp.float32)
        up_contribution = adapter_scale * lax.dot_general(upstream_gradient_rows, low_rank_rows, (((0,), (0,)), ((), ())), preferred_element_type=jnp.float32)
        sum_down = lax.dynamic_update_slice_in_dim(sum_down, lax.dynamic_slice_in_dim(sum_down, start, RANK, 1) + term_down, start, 1)
        sum_up = lax.dynamic_update_slice_in_dim(sum_up, lax.dynamic_slice_in_dim(sum_up, start, RANK, 1) + up_contribution, start, 1)
        return ((sum_down, sum_up), (adapter_branch, back_side))
    start_down = jnp.zeros(down_factor.shape, jnp.float32)
    start_up = jnp.zeros(up_factor.shape, jnp.float32)
    (grad_down, grad_up), (adapter_branch, back_side) = lax.scan(block_step, (start_down, start_up), (normalized_blocks, upstream_blocks, tenant))
    frozen_output = jnp.dot(normed, value_weight, preferred_element_type=jnp.float32)
    adapted_values = (frozen_output + adapter_scale * adapter_branch.reshape(-1, VALUE_HEAD_WIDTH)).astype(jnp.bfloat16)
    back = jnp.dot(upstream, value_weight.T, preferred_element_type=jnp.float32) + back_side.reshape(-1, D)
    gained = norm_gain * back
    inner = lax.optimization_barrier(jnp.sum(gained * wide_tokens, axis=1, keepdims=True))
    grad_tokens = (inverse * gained - wide_tokens * (inverse * inverse * inverse) * inner / D).astype(jnp.bfloat16)
    return (adapted_values, grad_tokens, grad_down, grad_up)
```

```python
import functools

import jax
import jax.numpy as jnp
import numpy as np
from jax import lax
from jax.experimental import pallas as pl
from jax.experimental.pallas import tpu as pltpu
from jax.sharding import Mesh
from jax.sharding import PartitionSpec as P

RANK = 64
BLK = 64

adapter_scale = 0.5
norm_eps = 1e-05


def over_chips(value, mask):
    chips = lax.axis_size("chip")
    return lax.ppermute(value, "chip", [(i, i ^ mask) for i in range(chips)])


def over_cores(value):
    return lax.ppermute(value, "core", [(0, 1), (1, 0)])


def slot_masks(chips):
    masks = [0]
    step = chips // 2
    while step:
        masks = masks + [m ^ step for m in masks]
        step //= 2
    return masks


def gather_over_chips(mine, chips):
    held, beside = mine, [over_chips(mine, 1)]
    step = chips // 2
    while step > 1:
        arrived = over_chips(held, step)
        beside.append(over_chips(arrived, 1))
        held = jnp.concatenate([held, arrived])
        step //= 2
    return jnp.concatenate([held] + beside)


def sum_over_chips(parts, chips):
    step = 1
    while step < chips:
        half = parts.shape[0] // 2
        arrived = over_chips(parts[half:].astype(jnp.bfloat16), step)
        parts = parts[:half] + arrived.astype(jnp.float32)
        step *= 2
    return parts[0]


def factor_grad_kernel(blocks, scale, tenant_ref, rows_ref, update_ref, out_ref):
    out_ref[...] = jnp.zeros_like(out_ref)
    lane = lax.broadcasted_iota(jnp.int32, (BLK, 2 * RANK), 1)

    def step(b, carry):
        adapter = tenant_ref[b]
        tokens = pl.ds(pl.multiple_of(b * BLK, BLK), BLK)
        update = update_ref[tokens, :]
        update = jnp.where(lane // RANK == adapter % 2, update, jnp.zeros_like(update))
        term = lax.dot_general(
            rows_ref[tokens, :], update, (((0,), (0,)), ((), ())), preferred_element_type=jnp.float32
        )
        columns = pl.ds(pl.multiple_of((adapter // 2) * 2 * RANK, 2 * RANK), 2 * RANK)
        out_ref[:, columns] += scale * term
        return carry

    lax.fori_loop(0, blocks, step, 0)


def factor_grad(rows, update, tenants, width, scale):
    blocks = tenants.shape[0]
    vmem = pl.BlockSpec(memory_space=pltpu.VMEM)
    return pl.pallas_call(
        functools.partial(factor_grad_kernel, blocks, scale),
        out_shape=jax.ShapeDtypeStruct((rows.shape[1], width), jnp.float32),
        in_specs=[pl.BlockSpec(memory_space=pltpu.SMEM), vmem, vmem],
        out_specs=vmem,
        compiler_params=pltpu.CompilerParams(vmem_limit_bytes=40 * 1024 * 1024),
        cost_estimate=pl.CostEstimate(
            flops=2 * rows.size * 2 * RANK,
            bytes_accessed=2 * rows.size + 4 * rows.shape[1] * width,
            transcendentals=0,
        ),
    )(tenants, rows, jnp.concatenate([update, update], axis=1))


def token_grad_kernel(
    slots, width, features, chip_ref, tokens_ref, gain_ref, inverse_ref, back_ref, out_ref, total
):
    inverse = inverse_ref[...]
    total[...] = jnp.zeros_like(total)

    def columns_of(s):
        return pl.ds(pl.multiple_of(chip_ref[s] * width, width), width)

    def add(s, carry):
        columns = columns_of(s)
        gained = gain_ref[:, columns] * back_ref[s].astype(jnp.float32)
        wide = tokens_ref[:, columns].astype(jnp.float32)
        total[...] += jnp.sum(gained * wide, axis=1, keepdims=True)
        return carry

    lax.fori_loop(0, slots, add, 0)
    cubed = inverse * inverse * inverse
    inner = total[...] / features

    def write(s, carry):
        columns = columns_of(s)
        gained = gain_ref[:, columns] * back_ref[s].astype(jnp.float32)
        wide = tokens_ref[:, columns].astype(jnp.float32)
        out_ref[:, columns] = (inverse * gained - wide * cubed * inner).astype(out_ref.dtype)
        return carry

    lax.fori_loop(0, slots, write, 0)


def token_grad(chip_of_slot, tokens, gain, inverse, back):
    slots, rows, width = back.shape
    features = tokens.shape[1]
    vmem = pl.BlockSpec(memory_space=pltpu.VMEM)
    return pl.pallas_call(
        functools.partial(token_grad_kernel, slots, width, features),
        out_shape=jax.ShapeDtypeStruct(tokens.shape, tokens.dtype),
        in_specs=[pl.BlockSpec(memory_space=pltpu.SMEM), vmem, vmem, vmem, vmem],
        out_specs=vmem,
        scratch_shapes=[pltpu.VMEM((rows, 1), jnp.float32)],
        compiler_params=pltpu.CompilerParams(vmem_limit_bytes=32 * 1024 * 1024),
        cost_estimate=pl.CostEstimate(
            flops=10 * tokens.size, bytes_accessed=6 * tokens.size, transcendentals=0
        ),
    )(chip_of_slot, tokens, gain, inverse, back)


def on_device(tokens, upstream, norm_gain, value_weight, down_factor, up_factor, tenant):
    chips = lax.axis_size("chip")
    chip, core = lax.axis_index("chip"), lax.axis_index("core")
    masks = slot_masks(chips)
    chip_of_slot = chip ^ jnp.asarray(masks, jnp.int32)
    slot_of_chip = jnp.asarray(np.argsort(masks), jnp.int32)[chip ^ jnp.arange(chips, dtype=jnp.int32)]

    token_rows, features = tokens.shape
    blocks = token_rows // BLK
    value_width = upstream.shape[1]
    adapters = down_factor.shape[1] // RANK
    width = features // chips
    value_rows = up_factor.shape[0]

    tenants = tenant.reshape(chips, 2, blocks)[chip_of_slot]
    tenants_mine, tenants_other = tenants[:, core].reshape(-1), tenants[:, 1 - core].reshape(-1)

    upstream_all = gather_over_chips(upstream, chips)

    def both_cores(mine):
        other = over_cores(mine)
        pair = jnp.stack([jnp.where(core == 0, mine, other), jnp.where(core == 0, other, mine)])
        return pair.reshape((2 * mine.shape[0],) + mine.shape[1:])

    weight = both_cores(value_weight)
    down = both_cores(down_factor)

    up_table = jnp.take(
        up_factor.reshape(value_rows, adapters, RANK), tenant, axis=1, mode="clip"
    ).reshape(value_rows, -1)
    up_mine = lax.all_to_all(up_table, ("chip", "core"), split_axis=1, concat_axis=0, tiled=True)
    up_blocks = up_mine.reshape(value_width, blocks, RANK)

    wide_tokens = tokens.astype(jnp.float32)
    inverse = lax.rsqrt(jnp.mean(wide_tokens * wide_tokens, axis=1, keepdims=True) + norm_eps)
    normed = (wide_tokens * inverse * norm_gain).astype(jnp.bfloat16)

    def columns_for(mask):
        return lax.dynamic_slice_in_dim(normed, (chip ^ mask) * width, width, 1)

    arrived = [over_chips(columns_for(m), m) if m else columns_for(m) for m in masks]
    normed_all = jnp.concatenate(arrived)

    upstream_blocks = upstream.reshape(blocks, BLK, value_width)
    mixed_output = jnp.einsum("bkv,vbr->bkr", upstream_blocks, up_blocks, preferred_element_type=jnp.float32)
    scaled_mine = (adapter_scale * mixed_output).astype(jnp.bfloat16).reshape(token_rows, RANK)
    scaled_all = lax.all_gather(scaled_mine, ("chip", "core"), axis=0)
    scaled_all = scaled_all.reshape(chips, 2, token_rows, RANK)[chip_of_slot]
    scaled_core = scaled_all[:, core].reshape(-1, RANK)
    scaled_other = scaled_all[:, 1 - core].reshape(-1, RANK)

    down_table = jnp.take(down.reshape(width, adapters, RANK), tenants_mine, axis=1, mode="clip")
    core_blocks = tenants_mine.shape[0]

    back = lax.dot_general(
        upstream_all, weight, (((1,), (1,)), ((), ())), preferred_element_type=jnp.float32
    )
    back = back + jnp.einsum(
        "pvq,opq->pvo",
        scaled_core.reshape(core_blocks, BLK, RANK),
        down_table,
        preferred_element_type=jnp.float32,
    ).reshape(-1, width)
    back = back.astype(jnp.bfloat16).reshape(chips, token_rows, width)
    back_mine = jnp.stack([over_chips(back[s], m) if m else back[s] for s, m in enumerate(masks)])

    values = jnp.dot(normed_all, weight, preferred_element_type=jnp.float32)
    values = sum_over_chips(values.reshape(chips, token_rows, value_width), chips)
    low = jnp.einsum(
        "yci,iya->yca",
        normed_all.reshape(core_blocks, BLK, width),
        down_table,
        preferred_element_type=jnp.float32,
    ).reshape(chips, token_rows, RANK)
    low = lax.psum(low[slot_of_chip], "chip").astype(jnp.bfloat16)
    low_mine = lax.dynamic_index_in_dim(low, chip, 0, keepdims=False).reshape(blocks, BLK, RANK)
    adapter_branch = jnp.einsum(
        "bkr,vbr->bkv", low_mine, up_blocks, preferred_element_type=jnp.float32
    ).reshape(token_rows, value_width)
    adapted_values = (values + adapter_scale * adapter_branch).astype(jnp.bfloat16)

    tenants_both = jnp.concatenate([tenants_mine, tenants_other])

    def my_columns(value, first, count):
        kept = lax.dynamic_slice_in_dim(value, first + core * count, count, 1)
        sent = lax.dynamic_slice_in_dim(value, first + (1 - core) * count, count, 1)
        return jnp.concatenate([kept, over_cores(sent)])

    grad_down = factor_grad(
        my_columns(normed_all, 0, width // 2),
        jnp.concatenate([scaled_core, scaled_other]),
        tenants_both,
        adapters * RANK,
        1.0,
    )
    low_slots = low[chip_of_slot].reshape(-1, RANK)
    grad_up = factor_grad(
        my_columns(upstream_all, chip * 2 * value_rows, value_rows),
        jnp.concatenate([low_slots, over_cores(low_slots)]),
        tenants_both,
        adapters * RANK,
        adapter_scale,
    )

    grad_tokens = token_grad(chip_of_slot, tokens, norm_gain.reshape(1, -1), inverse, back_mine)
    return (adapted_values, grad_tokens, grad_down, grad_up)


def solution(mesh):
    groups, shards = mesh.shape["groups"], mesh.shape["fsdp"]
    chip_mesh = Mesh(mesh.devices.reshape(groups, shards // 2, 2), ("groups", "chip", "core"))
    own = ("chip", "core")
    everywhere = P(("groups",) + own, None)
    in_specs = (everywhere, everywhere, P(), P(own, None), P(own, None), P(own, None), P("groups"))
    out_specs = (everywhere,) * 4
    return jax.shard_map(
        on_device, mesh=chip_mesh, in_specs=in_specs, out_specs=out_specs, check_vma=False
    )
```

```python
import functools

import jax
import jax.numpy as jnp
from jax import lax
from jax.experimental import pallas as pl
from jax.experimental.pallas import tpu as pltpu
from jax.sharding import Mesh
from jax.sharding import PartitionSpec as P

RANK = 64
BLK = 64

adapter_scale = 0.5
norm_eps = 1e-05


def over_chips(value, mask):
    chips = lax.axis_size("chip")
    return lax.ppermute(value, "chip", [(i, i ^ mask) for i in range(chips)])


def over_cores(value):
    return lax.ppermute(value, "core", [(0, 1), (1, 0)])


def near_masks(chips):
    masks, step = [0], chips // 4
    while step:
        masks = masks + [m ^ step for m in masks]
        step //= 2
    return masks


def slot_masks(chips):
    near = near_masks(chips)
    return near + [m ^ (chips // 2) for m in near]


def gather_over_chips(mine, chips):
    held, masks = mine, [0]
    pieces = [(mine, [0]), (over_chips(mine, 1), [1])]
    step = chips // 2
    while step > 1:
        arrived, arrived_masks = over_chips(held, step), [m ^ step for m in masks]
        pieces.append((arrived, arrived_masks))
        pieces.append((over_chips(arrived, 1), [m ^ 1 for m in arrived_masks]))
        held, masks = jnp.concatenate([held, arrived]), masks + arrived_masks
        step //= 2
    return pieces


def gather_small(mine, chips):
    near, step = mine, chips // 4
    far = over_chips(mine, chips // 2)
    held = jnp.stack([near, far])
    while step:
        held = jnp.concatenate([held, over_chips(held, step)], axis=1)
        step //= 2
    return held.reshape((-1,) + mine.shape[1:])


def packed(values, low):
    high = lax.reduce_precision(low, 8, 7)
    return jnp.concatenate([values, high, low - high], axis=-1).astype(jnp.bfloat16)


def unpacked(sent, value_width):
    sent = sent.astype(jnp.float32)
    low = sent[..., value_width : value_width + RANK] + sent[..., value_width + RANK :]
    return sent[..., :value_width], low


def sum_over_chips(sends, values, low, chips):
    value_width = values[0].shape[-1]
    values, low = list(values), list(low)
    for side in (1, 0):
        step, sent = 1, sends[side]
        while True:
            more_values, more_low = unpacked(over_chips(sent, step), value_width)
            values[side] = values[side] + more_values
            low[side] = low[side] + more_low
            half = values[side].shape[0] // 2
            if not half:
                break
            sent = packed(values[side][half:], low[side][half:])
            values[side], low[side] = values[side][:half], low[side][:half]
            step *= 2
    more_values, more_low = unpacked(over_chips(packed(values[1], low[1]), chips // 2), value_width)
    return (values[0] + more_values)[0], (low[0] + more_low)[0]


def adapter_columns(adapter):
    return pl.ds(pl.multiple_of((adapter // 2) * 2 * RANK, 2 * RANK), 2 * RANK)


def back_kernel(masks, pieces, blocks, scalar_ref, tenant_ref, weight_ref, down_ref, scaled_ref, *refs):
    upstream_refs, out_ref = refs[:-1], refs[-1]
    lane = lax.broadcasted_iota(jnp.int32, (BLK, 2 * RANK), 1)
    rows = blocks * BLK
    contract = (((1,), (1,)), ((), ()))
    for upstream_ref, piece_masks in zip(upstream_refs, pieces):
        product = lax.dot_general(
            upstream_ref[...], weight_ref[...], contract, preferred_element_type=jnp.float32
        )
        for at, mask in enumerate(piece_masks):
            slot = masks.index(mask)
            for b in range(blocks):
                adapter = tenant_ref[slot * blocks + b]
                update = scaled_ref[slot * rows + b * BLK : slot * rows + (b + 1) * BLK, :]
                update = jnp.where(lane // RANK == adapter % 2, update, jnp.zeros_like(update))
                term = lax.dot_general(
                    update, down_ref[:, adapter_columns(adapter)], contract, preferred_element_type=jnp.float32
                )
                first = at * rows + b * BLK
                out_ref[scalar_ref[0] ^ mask, b * BLK : (b + 1) * BLK, :] = (
                    product[first : first + BLK] + term
                ).astype(out_ref.dtype)


def back_products(chip, masks, tenants, weight, down, scaled, pieces, token_rows):
    vmem, smem = pl.BlockSpec(memory_space=pltpu.VMEM), pl.BlockSpec(memory_space=pltpu.SMEM)
    width = weight.shape[0]
    slots = len(masks)
    return pl.pallas_call(
        functools.partial(back_kernel, masks, [m for _, m in pieces], token_rows // BLK),
        out_shape=jax.ShapeDtypeStruct((slots, token_rows, width), jnp.bfloat16),
        in_specs=[smem, smem] + [vmem] * (3 + len(pieces)),
        out_specs=vmem,
        compiler_params=pltpu.CompilerParams(vmem_limit_bytes=48 * 1024 * 1024),
        cost_estimate=pl.CostEstimate(
            flops=2 * slots * token_rows * width * weight.shape[1],
            bytes_accessed=2 * (weight.size + down.size + 2 * slots * token_rows * width),
            transcendentals=0,
        ),
    )(chip.reshape(1), tenants, weight, down, scaled, *[rows for rows, _ in pieces])


def value_kernel(slots, blocks, core_ref, tenant_ref, weight_ref, down_ref, *refs):
    normed_refs = refs[:slots]
    sides = (refs[slots : slots + 3], refs[slots + 3 : slots + 6])
    mine_ref, other_ref = refs[slots + 6 :]
    rows, width = normed_refs[0].shape
    half, kept = width // 2, slots // 4
    value_width = weight_ref.shape[1]
    for slot in range(slots):
        normed = normed_refs[slot][...]
        sent_ref, values_ref, low_ref = sides[slot // (slots // 2)]
        at = slot % (slots // 2)
        values = jnp.dot(normed, weight_ref[...], preferred_element_type=jnp.float32)
        low = []
        for b in range(blocks):
            adapter = tenant_ref[slot * blocks + b]
            both = jnp.dot(
                normed[b * BLK : (b + 1) * BLK],
                down_ref[:, adapter_columns(adapter)],
                preferred_element_type=jnp.float32,
            )
            low.append(jnp.where(adapter % 2 == 0, both[:, :RANK], both[:, RANK:]))
        low = jnp.concatenate(low, axis=0)
        if at < kept:
            values_ref[at] = values
            low_ref[at] = low
        else:
            high = low.astype(jnp.bfloat16)
            rest = (low - high.astype(jnp.float32)).astype(jnp.bfloat16)
            sent_ref[at - kept, :, :value_width] = values.astype(jnp.bfloat16)
            sent_ref[at - kept, :, value_width:] = jnp.concatenate([high, rest], axis=1)
        first, second = normed[:, :half], normed[:, half:]
        mine_ref[slot * rows : (slot + 1) * rows, :] = jnp.where(core_ref[0] == 0, first, second)
        other_ref[slot * rows : (slot + 1) * rows, :] = jnp.where(core_ref[0] == 0, second, first)


def value_products(core, tenants, weight, down, normed):
    vmem, smem = pl.BlockSpec(memory_space=pltpu.VMEM), pl.BlockSpec(memory_space=pltpu.SMEM)
    slots = len(normed)
    rows, width = normed[0].shape
    value_width = weight.shape[1]
    side = [
        jax.ShapeDtypeStruct((slots // 4, rows, value_width + 2 * RANK), jnp.bfloat16),
        jax.ShapeDtypeStruct((slots // 4, rows, value_width), jnp.float32),
        jax.ShapeDtypeStruct((slots // 4, rows, RANK), jnp.float32),
    ]
    half = jax.ShapeDtypeStruct((slots * rows, width // 2), jnp.bfloat16)
    return pl.pallas_call(
        functools.partial(value_kernel, slots, rows // BLK),
        out_shape=side + side + [half, half],
        in_specs=[smem, smem] + [vmem] * (2 + slots),
        out_specs=[vmem] * 8,
        compiler_params=pltpu.CompilerParams(vmem_limit_bytes=56 * 1024 * 1024),
        cost_estimate=pl.CostEstimate(
            flops=2 * slots * rows * width * value_width,
            bytes_accessed=2 * (weight.size + down.size + 5 * slots * rows * width),
            transcendentals=0,
        ),
    )(core.reshape(1), tenants, weight, down, *normed)


def factor_grad_kernel(blocks, scale, tenant_ref, *refs):
    out_ref = refs[-1]
    out_ref[...] = jnp.zeros_like(out_ref)
    lane = lax.broadcasted_iota(jnp.int32, (BLK, 2 * RANK), 1)

    for which in range(2):
        rows_ref, update_ref = refs[2 * which], refs[2 * which + 1]

        def step(b, carry, rows_ref=rows_ref, update_ref=update_ref, which=which):
            adapter = tenant_ref[which * blocks + b]
            tokens = pl.ds(pl.multiple_of(b * BLK, BLK), BLK)
            update = update_ref[tokens, :]
            update = jnp.where(lane // RANK == adapter % 2, update, jnp.zeros_like(update))
            term = lax.dot_general(
                rows_ref[tokens, :], update, (((0,), (0,)), ((), ())), preferred_element_type=jnp.float32
            )
            out_ref[:, adapter_columns(adapter)] += scale * term
            return carry

        lax.fori_loop(0, blocks, step, 0)


def factor_grad(rows, update, other_rows, other_update, tenants, width, scale):
    vmem = pl.BlockSpec(memory_space=pltpu.VMEM)
    return pl.pallas_call(
        functools.partial(factor_grad_kernel, tenants.shape[0] // 2, scale),
        out_shape=jax.ShapeDtypeStruct((rows.shape[1], width), jnp.float32),
        in_specs=[pl.BlockSpec(memory_space=pltpu.SMEM)] + [vmem] * 4,
        out_specs=vmem,
        compiler_params=pltpu.CompilerParams(vmem_limit_bytes=40 * 1024 * 1024),
        cost_estimate=pl.CostEstimate(
            flops=4 * rows.size * 2 * RANK,
            bytes_accessed=4 * rows.size + 4 * rows.shape[1] * width,
            transcendentals=0,
        ),
    )(tenants, rows, update, other_rows, other_update)


def token_grad_kernel(slots, width, features, tokens_ref, gain_ref, inverse_ref, back_ref, out_ref):
    inverse = inverse_ref[...]
    total = jnp.zeros_like(inverse)
    for s in range(slots):
        columns = slice(s * width, (s + 1) * width)
        gained = gain_ref[:, columns] * back_ref[s].astype(jnp.float32)
        wide = tokens_ref[:, columns].astype(jnp.float32)
        total += jnp.sum(gained * wide, axis=1, keepdims=True)
    cubed = inverse * inverse * inverse
    inner = total / features
    for s in range(slots):
        columns = slice(s * width, (s + 1) * width)
        gained = gain_ref[:, columns] * back_ref[s].astype(jnp.float32)
        wide = tokens_ref[:, columns].astype(jnp.float32)
        out_ref[:, columns] = (inverse * gained - wide * cubed * inner).astype(out_ref.dtype)


def token_grad(tokens, gain, inverse, back):
    slots, rows, width = back.shape
    vmem = pl.BlockSpec(memory_space=pltpu.VMEM)
    return pl.pallas_call(
        functools.partial(token_grad_kernel, slots, width, tokens.shape[1]),
        out_shape=jax.ShapeDtypeStruct(tokens.shape, tokens.dtype),
        in_specs=[vmem] * 4,
        out_specs=vmem,
        compiler_params=pltpu.CompilerParams(vmem_limit_bytes=32 * 1024 * 1024),
        cost_estimate=pl.CostEstimate(
            flops=10 * tokens.size, bytes_accessed=6 * tokens.size, transcendentals=0
        ),
    )(tokens, gain, inverse, back)


def on_device(tokens, upstream, norm_gain, value_weight, down_factor, up_factor, tenant):
    chips = lax.axis_size("chip")
    chip, core = lax.axis_index("chip"), lax.axis_index("core")
    masks = slot_masks(chips)
    chip_of_slot = chip ^ jnp.asarray(masks, jnp.int32)

    token_rows, features = tokens.shape
    blocks = token_rows // BLK
    value_width = upstream.shape[1]
    adapters = down_factor.shape[1] // RANK
    width = features // chips
    value_rows = up_factor.shape[0]

    tenants = tenant.reshape(chips, 2, blocks)[chip_of_slot]
    tenants_mine, tenants_other = tenants[:, core].reshape(-1), tenants[:, 1 - core].reshape(-1)
    tenants_both = jnp.concatenate([tenants_mine, tenants_other])

    upstream_pieces = gather_over_chips(upstream, chips)

    def both_cores(mine):
        other = over_cores(mine)
        pair = jnp.stack([jnp.where(core == 0, mine, other), jnp.where(core == 0, other, mine)])
        return pair.reshape((2 * mine.shape[0],) + mine.shape[1:])

    weight = both_cores(value_weight)
    down = both_cores(down_factor)

    up_table = jnp.take(
        up_factor.reshape(value_rows, adapters, RANK), tenant, axis=1, mode="clip"
    ).reshape(value_rows, -1)
    up_mine = lax.all_to_all(up_table, ("chip", "core"), split_axis=1, concat_axis=0, tiled=True)
    up_blocks = up_mine.reshape(value_width, blocks, RANK)

    wide_tokens = tokens.astype(jnp.float32)
    inverse = lax.rsqrt(jnp.mean(wide_tokens * wide_tokens, axis=1, keepdims=True) + norm_eps)
    normed = (wide_tokens * inverse * norm_gain).astype(jnp.bfloat16)

    def columns_for(mask):
        return lax.dynamic_slice_in_dim(normed, (chip ^ mask) * width, width, 1)

    arrived = {m: over_chips(columns_for(m), m) if m else columns_for(m) for m in reversed(masks)}
    arrived = [arrived[m] for m in masks]

    upstream_blocks = upstream.reshape(blocks, BLK, value_width)
    mixed_output = jnp.einsum("bkv,vbr->bkr", upstream_blocks, up_blocks, preferred_element_type=jnp.float32)
    scaled_mine = (adapter_scale * mixed_output).astype(jnp.bfloat16).reshape(token_rows, RANK)
    scaled = gather_small(jnp.concatenate([scaled_mine, scaled_mine], axis=1), chips)
    scaled_other = over_cores(scaled)

    back = back_products(chip, masks, tenants_mine, weight, down, scaled, upstream_pieces, token_rows)
    back_mine = lax.all_to_all(back, "chip", split_axis=0, concat_axis=0, tiled=True)
    arrived, back = lax.optimization_barrier((arrived, back))

    products = value_products(core, tenants_mine, weight, down, arrived)
    (near_sent, near_values, near_low, far_sent, far_values, far_low, normed_mine, normed_sent) = products
    values, low = sum_over_chips(
        (near_sent, far_sent), (near_values, far_values), (near_low, far_low), chips
    )
    low_mine = low.astype(jnp.bfloat16)
    adapter_branch = jnp.einsum(
        "bkr,vbr->bkv", low_mine.reshape(blocks, BLK, RANK), up_blocks, preferred_element_type=jnp.float32
    ).reshape(token_rows, value_width)
    adapted_values = (values + adapter_scale * adapter_branch).astype(jnp.bfloat16)

    grad_down = factor_grad(
        normed_mine, scaled, over_cores(normed_sent), scaled_other, tenants_both, adapters * RANK, 1.0
    )
    by_mask = {}
    for rows, piece_masks in upstream_pieces:
        for at, mask in enumerate(piece_masks):
            by_mask[mask] = rows[at * token_rows : (at + 1) * token_rows]

    def upstream_columns(whose):
        first = chip * 2 * value_rows + whose * value_rows
        return jnp.concatenate([lax.dynamic_slice_in_dim(by_mask[m], first, value_rows, 1) for m in masks])

    low_core = gather_small(jnp.concatenate([low_mine, low_mine], axis=1), chips)
    grad_up = factor_grad(
        upstream_columns(core),
        low_core,
        over_cores(upstream_columns(1 - core)),
        over_cores(low_core),
        tenants_both,
        adapters * RANK,
        adapter_scale,
    )

    grad_tokens = token_grad(tokens, norm_gain.reshape(1, -1), inverse, back_mine)
    return (adapted_values, grad_tokens, grad_down, grad_up)


def solution(mesh):
    groups, shards = mesh.shape["groups"], mesh.shape["fsdp"]
    chip_mesh = Mesh(mesh.devices.reshape(groups, shards // 2, 2), ("groups", "chip", "core"))
    own = ("chip", "core")
    everywhere = P(("groups",) + own, None)
    in_specs = (everywhere, everywhere, P(), P(own, None), P(own, None), P(own, None), P("groups"))
    out_specs = (everywhere,) * 4
    return jax.shard_map(
        on_device, mesh=chip_mesh, in_specs=in_specs, out_specs=out_specs, check_vma=False
    )
```

```python
import functools

import jax
import jax.numpy as jnp
from jax import lax
from jax.experimental import pallas as pl
from jax.experimental.pallas import tpu as pltpu
from jax.sharding import Mesh
from jax.sharding import PartitionSpec as P

RANK = 64
BLK = 64
PAIR = 2 * RANK

adapter_scale = 0.5
norm_eps = 1e-05

QUICK = pl.CostEstimate(flops=1, bytes_accessed=1, transcendentals=0)
MIB = 1024 * 1024


def over_line(value, mask):
    size = lax.axis_size("line")
    return lax.ppermute(value, "line", [(i, i ^ mask) for i in range(size)])


def over_pair(value):
    return lax.ppermute(value, "pair", [(0, 1), (1, 0)])


def over_cores(value):
    return lax.ppermute(value, "core", [(0, 1), (1, 0)])


def after(value, *others):
    return lax.optimization_barrier((value,) + others)[0]


def swap_rest(mine, for_core, crossed):
    beside = over_cores(jnp.stack([for_core, crossed[1]]))
    return [mine, beside[0], crossed[0], beside[1]]


def order_kernel(place_ref, *refs):
    for r, ref in enumerate(refs[:-1]):
        refs[-1][place_ref[0] ^ r] = ref[...]


def in_order(parts, place):
    shape = jax.ShapeDtypeStruct((4,) + parts[0].shape, parts[0].dtype)
    ordered = call(order_kernel, shape, [place.reshape(1)], parts, 24)
    return ordered.reshape((-1,) + parts[0].shape[1:])


def gather_line(held):
    size = lax.axis_size("line")
    pieces, slots, step = [(held, [0, size // 2])], [0, size // 2], size // 4
    while step:
        arrived = over_line(held, step)
        more = [s ^ step for s in slots]
        pieces.append((arrived, more))
        slots, step = slots + more, step // 2
        held = jnp.concatenate([held, arrived]) if step else held
    return pieces


def in_slots(pieces):
    rows = pieces[0][0].shape[0] // 2
    found = {m: p[i * rows : (i + 1) * rows] for p, ms in pieces for i, m in enumerate(ms)}
    return jnp.concatenate([found[m] for m in range(len(found))])


def two_terms(low):
    high = lax.reduce_precision(low, 8, 7)
    return jnp.concatenate([high, low - high], axis=-1).astype(jnp.bfloat16)


def one_term(sent):
    sent = sent.astype(jnp.float32)
    return sent[..., :RANK] + sent[..., RANK:]


def adapter_columns(adapter):
    return pl.ds(pl.multiple_of((adapter // 2) * PAIR, PAIR), PAIR)


def adapter_half(both, adapter):
    return jnp.where(adapter % 2 == 0, both[:, :RANK], both[:, RANK:])


def on_diagonal(update):
    row = lax.broadcasted_iota(jnp.int32, update.shape, 0) // BLK
    column = lax.broadcasted_iota(jnp.int32, update.shape, 1) // RANK
    return jnp.where(row == column, update, jnp.zeros_like(update))


def call(kernel, out_shape, scalars, arrays, limit):
    vmem, smem = pl.BlockSpec(memory_space=pltpu.VMEM), pl.BlockSpec(memory_space=pltpu.SMEM)
    return pl.pallas_call(
        kernel,
        out_shape=out_shape,
        in_specs=[smem] * len(scalars) + [vmem] * len(arrays),
        out_specs=jax.tree.map(lambda _: vmem, out_shape),
        cost_estimate=QUICK,
        compiler_params=pltpu.CompilerParams(vmem_limit_bytes=60 * MIB),
    )(*scalars, *arrays)


def first_kernel(slots, wanted, line_ref, tenant_ref, tokens_ref, gain_ref, up_ref, table_ref, inverse_ref, *normed_refs):
    columns_kernel(wanted, tenant_ref, up_ref, table_ref)
    features = tokens_ref.shape[1]
    width = features // slots
    total = jnp.zeros(inverse_ref.shape, jnp.float32)
    for s in range(slots):
        wide = tokens_ref[:, s * width : (s + 1) * width].astype(jnp.float32)
        total += jnp.sum(wide * wide, axis=1, keepdims=True)
    inverse = lax.rsqrt(total / features + norm_eps)
    inverse_ref[...] = inverse
    for s in range(slots):
        columns = pl.ds(pl.multiple_of((line_ref[0] ^ s) * width, width), width)
        wide = tokens_ref[:, columns].astype(jnp.float32)
        normed_refs[s][...] = (wide * inverse * gain_ref[:, columns]).astype(jnp.bfloat16)


def norm_and_up(line, tenant, tokens, gain, up_factor, wanted):
    rows, features = tokens.shape
    slots = len(wanted) // 4
    shapes = [
        jax.ShapeDtypeStruct((len(wanted), up_factor.shape[0], len(wanted[0]) * RANK), up_factor.dtype),
        jax.ShapeDtypeStruct((rows, 1), jnp.float32),
    ] + [jax.ShapeDtypeStruct((rows, features // slots), jnp.bfloat16)] * slots
    return call(
        functools.partial(first_kernel, slots, wanted), shapes, [line, tenant], [tokens, gain, up_factor], 40
    )


def columns_kernel(wanted, tenant_ref, factor_ref, *out_refs):
    refs = [r.at[i] for r in out_refs for i in range(r.shape[0])]
    for d, blocks in enumerate(wanted):
        for first in range(0, len(blocks), 2):
            parts = []
            for b in blocks[first : first + 2]:
                adapter = tenant_ref[b]
                parts.append(adapter_half(factor_ref[:, adapter_columns(adapter)], adapter))
            refs[d][:, first * RANK : first * RANK + PAIR] = jnp.concatenate(parts, axis=1)


def columns_of(wanted, tenants, factor, stacks):
    shapes = [
        jax.ShapeDtypeStruct((n, factor.shape[0], len(wanted[0]) * RANK), factor.dtype) for n in stacks
    ]
    return call(functools.partial(columns_kernel, wanted), shapes, [tenants], [factor], 24)


def scaled_kernel(upstream_ref, far_ref, up_ref, out_ref):
    rows = upstream_ref.shape[0]
    for which, ref in enumerate((upstream_ref, far_ref)):
        mixed = jnp.dot(ref[...], up_ref[...], preferred_element_type=jnp.float32)
        for b in range(rows // BLK):
            at = which * rows + b * BLK
            block = mixed[b * BLK : (b + 1) * BLK, at // BLK * RANK : (at // BLK + 1) * RANK]
            scaled = (adapter_scale * block).astype(out_ref.dtype)
            out_ref[at : at + BLK, :] = jnp.concatenate([scaled, scaled], axis=1)


def back_kernel(pieces, rows, weight_ref, down_ref, scaled_ref, *refs):
    upstream_refs, out_refs = refs[: len(pieces)], refs[len(pieces) :]
    contract = (((1,), (1,)), ((), ()))
    for upstream_ref, slots in zip(upstream_refs, pieces):
        product = lax.dot_general(
            upstream_ref[...], weight_ref[...], contract, preferred_element_type=jnp.float32
        )
        for at, slot in enumerate(slots):
            for r in range(0, rows, 2 * BLK):
                first, held = at * rows + r, slot * rows + r
                column = held // BLK * RANK
                term = lax.dot_general(
                    on_diagonal(scaled_ref[held : held + 2 * BLK, :]),
                    down_ref[:, column : column + PAIR],
                    contract,
                    preferred_element_type=jnp.float32,
                )
                out_refs[slot][r : r + 2 * BLK, :] = (product[first : first + 2 * BLK] + term).astype(jnp.bfloat16)


def value_kernel(slots, weight_ref, down_ref, *refs):
    normed_refs, (values_ref, low_ref, sent_ref) = refs[:slots], refs[slots:]
    value_width = weight_ref.shape[1]
    for slot in range(slots):
        normed = normed_refs[slot][...]
        rows = normed.shape[0]
        values = jnp.dot(normed, weight_ref[...], preferred_element_type=jnp.float32)
        low = []
        for b in range(rows // BLK):
            column = (slot * rows // BLK + b) // 2 * PAIR
            both = jnp.dot(
                normed[b * BLK : (b + 1) * BLK],
                down_ref[:, column : column + PAIR],
                preferred_element_type=jnp.float32,
            )
            low.append(both[:, b % 2 * RANK : (b % 2 + 1) * RANK])
        low = jnp.concatenate(low, axis=0)
        if slot % 2:
            high = low.astype(jnp.bfloat16)
            rest = (low - high.astype(jnp.float32)).astype(jnp.bfloat16)
            sent_ref[slot // 2, :, :value_width] = values.astype(jnp.bfloat16)
            sent_ref[slot // 2, :, value_width:] = jnp.concatenate([high, rest], axis=1)
        else:
            values_ref[slot // 2] = values
            low_ref[slot // 2] = low


def value_products(weight, down, normed):
    slots, rows = len(normed), normed[0].shape[0]
    half, value_width = slots // 2, weight.shape[1]
    shapes = [
        jax.ShapeDtypeStruct((half, rows, value_width), jnp.float32),
        jax.ShapeDtypeStruct((half, rows, RANK), jnp.float32),
        jax.ShapeDtypeStruct((half, rows, value_width + PAIR), jnp.bfloat16),
    ]
    return call(functools.partial(value_kernel, slots), shapes, [], [weight, down, *normed], 56)


def sum_over_line(values, low, crossed, waits):
    value_width, far, step = values.shape[-1], lax.axis_size("line") // 2, 2
    values = values + crossed[..., :value_width].astype(jnp.float32)
    low = low + one_term(crossed[..., value_width:])
    while step < far:
        low = low[::2] + one_term(over_line(two_terms(low[1::2]), step))
        values = values[::2] + over_line(values[1::2].astype(jnp.bfloat16), step).astype(jnp.float32)
        step *= 2
    low = low + one_term(over_line(after(two_terms(low), *waits), far))[::-1]
    return values[0] + over_line(values[1].astype(jnp.bfloat16), far).astype(jnp.float32), low


def terms_kernel(slots, scale, place_ref, update_ref, *refs):
    rows_refs, out_ref = refs[:slots], refs[slots]
    rows, width = rows_refs[0].shape
    shard = width // 4
    for slot in range(slots):
        for r in range(0, rows, 2 * BLK):
            first = slot * rows + r
            term = scale * lax.dot_general(
                rows_refs[slot][r : r + 2 * BLK, :],
                on_diagonal(update_ref[first : first + 2 * BLK, :]),
                (((0,), (0,)), ((), ())),
                preferred_element_type=jnp.float32,
            )
            term = term.astype(jnp.bfloat16)
            column = first // BLK * RANK
            for p in range(4):
                out_ref[place_ref[0] ^ p, :, column : column + PAIR] = term[p * shard : (p + 1) * shard]


def factor_terms(place, update, rows, scale):
    slots, (count, width) = len(rows), rows[0].shape
    shape = jax.ShapeDtypeStruct((4, width // 4, slots * count // BLK * RANK), jnp.bfloat16)
    return call(functools.partial(terms_kernel, slots, scale), shape, [place], [update, *rows], 48)


def owner_kernel(blocks, tenant_ref, *refs):
    out_ref = refs[-1]
    out_ref[...] = jnp.zeros_like(out_ref)
    lane = lax.broadcasted_iota(jnp.int32, (out_ref.shape[0], PAIR), 1) // RANK
    for r, terms_ref in enumerate(refs[:-1]):
        for first in range(0, blocks, 2):
            both = terms_ref[:, first * RANK : first * RANK + PAIR].astype(jnp.float32)
            turned = jnp.concatenate([both[:, RANK:], both[:, :RANK]], axis=1)
            for h in range(2):
                adapter = tenant_ref[r * blocks + first + h]
                side = adapter % 2
                term = jnp.where(side == h, both, turned)
                out_ref[:, adapter_columns(adapter)] += jnp.where(lane == side, term, jnp.zeros_like(term))


def owner_sums(tenants, terms, width):
    blocks = tenants.shape[1]
    shape = jax.ShapeDtypeStruct((terms[0].shape[0], width), jnp.float32)
    return call(functools.partial(owner_kernel, blocks), shape, [tenants.reshape(-1)], terms, 40)


def token_grad_kernel(slots, line_ref, tokens_ref, gain_ref, inverse_ref, *refs):
    back_refs, out_ref = refs[:-1], refs[-1]
    width = back_refs[0].shape[1]
    inverse = inverse_ref[...]
    total = jnp.zeros_like(inverse)

    def load(s):
        columns = pl.ds(pl.multiple_of((line_ref[0] ^ s) * width, width), width)
        gained = gain_ref[:, columns] * back_refs[s][...].astype(jnp.float32)
        return columns, gained, tokens_ref[:, columns].astype(jnp.float32)

    for s in range(slots):
        _, gained, wide = load(s)
        total += jnp.sum(gained * wide, axis=1, keepdims=True)
    cubed = inverse * inverse * inverse
    inner = total / tokens_ref.shape[1]
    for s in range(slots):
        columns, gained, wide = load(s)
        out_ref[:, columns] = (inverse * gained - wide * cubed * inner).astype(out_ref.dtype)


def on_device(tokens, upstream, norm_gain, value_weight, down_factor, up_factor, tenant):
    size, far = lax.axis_size("line"), lax.axis_size("line") // 2
    line, pair, core = lax.axis_index("line"), lax.axis_index("pair"), lax.axis_index("core")
    place = 2 * pair + core
    line_, place_ = line.reshape(1), place.reshape(1)
    rows = tokens.shape[0]
    blocks = rows // BLK
    value_width = upstream.shape[1]
    adapter_width = down_factor.shape[1]
    value_rows = up_factor.shape[0]
    gain = norm_gain.reshape(1, -1)

    tenants_of = tenant.reshape(size, 4, blocks)
    tenants = tenants_of[line ^ jnp.arange(size, dtype=jnp.int32)].transpose(1, 0, 2)
    tenants = tenants[place ^ jnp.arange(4, dtype=jnp.int32)].reshape(4, size * blocks)

    upstream_far = over_line(upstream, far)

    wanted = [
        [e * blocks + b for e in (d, d ^ (4 * far)) for b in range(blocks)] for d in range(4 * size)
    ]
    up_sent, inverse, *normed = norm_and_up(line_, tenant, tokens, gain, up_factor, wanted)
    arrived = [normed[0]] + [over_line(after(normed[s], upstream_far), s) for s in range(1, far + 1)]
    up_mine = lax.all_to_all(
        after(up_sent, upstream_far, over_cores(inverse)), ("line", "pair", "core"), split_axis=0, concat_axis=0, tiled=True
    )
    up_mine = up_mine.reshape(value_width, 2 * blocks * RANK)

    across = over_pair(value_weight)
    down_mine, down_core, down_pair = columns_of(
        [[r * size * blocks + b for b in range(size * blocks)] for r in range(4)],
        tenants.reshape(-1),
        after(down_factor, normed[0]),
        [1, 1, 2],
    )
    down_crossed = over_pair(down_pair)

    pieces = gather_line(jnp.concatenate([upstream, upstream_far]))
    scaled = call(
        scaled_kernel,
        jax.ShapeDtypeStruct((2 * rows, PAIR), jnp.bfloat16),
        [],
        [after(upstream, *arrived[1:], across, down_crossed, *[p for p, _ in pieces]), upstream_far, up_mine],
        16,
    )
    scaled = in_slots(gather_line(scaled))
    arrived += [over_line(after(normed[s], scaled), s) for s in range(far + 1, size)]
    across, down_crossed, scaled = lax.optimization_barrier((across, down_crossed, scaled))
    beside = over_cores(jnp.stack([value_weight, across]))
    weight = in_order([value_weight, beside[0], across, beside[1]], place)
    down = in_order(swap_rest(down_mine[0], down_core[0], down_crossed), place)

    back = call(
        functools.partial(back_kernel, [s for _, s in pieces], rows),
        [jax.ShapeDtypeStruct((rows, weight.shape[0]), jnp.bfloat16)] * size,
        [],
        [weight, down, scaled] + [p for p, _ in pieces],
        56,
    )
    half = rows // 2
    first = over_line(back[far][:half], far)

    values, low, sent = value_products(after(weight, back[0]), down, arrived)
    crossed = over_line(after(sent, first), 1)
    back_mine = {s: over_line(after(back[s], crossed), s) for s in range(1, far)}
    back_mine[0] = back[0]
    back_mine[far] = jnp.concatenate([first, over_line(after(back[far][half:], first), far)])
    for s in range(far + 1, size):
        back_mine[s] = over_line(after(back[s], first), s)
    back_mine = [back_mine[s] for s in range(size)]

    terms = factor_terms(place_, after(scaled, first), arrived, 1.0)
    terms = swap_rest(terms[0], terms[1], over_pair(terms[2:]))
    grad_down = owner_sums(tenants, terms, adapter_width)

    values, low = sum_over_line(values, low, crossed, back_mine[far : far + 1])
    low = low.astype(jnp.bfloat16)
    columns = [
        (lax.dynamic_slice_in_dim(p, line * 4 * value_rows, 4 * value_rows, 1), s)
        for p, s in pieces
    ]
    low_held = jnp.concatenate([low, low], axis=-1).reshape(2 * rows, PAIR)
    low_all = in_slots(gather_line(after(low_held, grad_down, *back_mine[far + 1 :])))
    terms = factor_terms(place_, low_all, [in_slots(columns)], adapter_scale)
    terms = swap_rest(terms[0], terms[1], over_pair(terms[2:]))
    grad_up = owner_sums(tenants, terms, adapter_width)

    adapter_branch = jnp.einsum(
        "bkr,vbr->bkv",
        low[0].reshape(blocks, BLK, RANK),
        up_mine[:, : blocks * RANK].reshape(value_width, blocks, RANK),
        preferred_element_type=jnp.float32,
    ).reshape(rows, value_width)
    adapted_values = (values + adapter_scale * adapter_branch).astype(jnp.bfloat16)

    grad_tokens = call(
        functools.partial(token_grad_kernel, size),
        jax.ShapeDtypeStruct(tokens.shape, tokens.dtype),
        [line_],
        [tokens, gain, after(inverse, grad_down, grad_up), *back_mine],
        32,
    )
    return (adapted_values, grad_tokens, grad_down, grad_up)


def solution(mesh):
    groups, shards = mesh.shape["groups"], mesh.shape["fsdp"]
    line_mesh = Mesh(mesh.devices.reshape(groups, shards // 4, 2, 2), ("groups", "line", "pair", "core"))
    own = ("line", "pair", "core")
    everywhere = P(("groups",) + own, None)
    in_specs = (everywhere, everywhere, P(), P(own, None), P(own, None), P(own, None), P("groups"))
    out_specs = (everywhere,) * 4
    return jax.shard_map(
        on_device, mesh=line_mesh, in_specs=in_specs, out_specs=out_specs, check_vma=False
    )
```

```python
import functools

import jax
import jax.numpy as jnp
from jax import lax
from jax.experimental import pallas as pl
from jax.experimental.pallas import tpu as pltpu
from jax.sharding import Mesh
from jax.sharding import PartitionSpec as P

RANK = 64
BLK = 64
PAIR = 2 * RANK

adapter_scale = 0.5
norm_eps = 1e-05

QUICK = pl.CostEstimate(flops=1, bytes_accessed=1, transcendentals=0)
MIB = 1024 * 1024


def over_line(value, mask):
    size = lax.axis_size("line")
    return lax.ppermute(value, "line", [(i, i ^ mask) for i in range(size)])


def over_pair(value):
    return lax.ppermute(value, "pair", [(0, 1), (1, 0)])


def over_cores(value):
    return lax.ppermute(value, "core", [(0, 1), (1, 0)])


def after(value, *others):
    return lax.optimization_barrier((value,) + others)[0]


def order_kernel(place_ref, mine_ref, beside_ref, across_ref, corner_ref, out_ref):
    for r, ref in enumerate((mine_ref, beside_ref, across_ref, corner_ref)):
        out_ref[place_ref[0] ^ r] = ref[...] if len(ref.shape) == 2 else ref[0]


def in_order(parts, place):
    rows, width = parts[0].shape
    shape = jax.ShapeDtypeStruct((4, rows, width), parts[0].dtype)
    return call(order_kernel, shape, [place.reshape(1)], parts).reshape(4 * rows, width)


def gather_line(held):
    size = lax.axis_size("line")
    pieces, slots, step = [(held, [0, size // 2])], [0, size // 2], size // 4
    while step:
        arrived = over_line(held, step)
        more = [s ^ step for s in slots]
        pieces.append((arrived, more))
        slots, step = slots + more, step // 2
        held = jnp.concatenate([held, arrived]) if step else held
    return pieces


def in_slots(pieces):
    rows = pieces[0][0].shape[0] // 2
    found = {m: p[i * rows : (i + 1) * rows] for p, ms in pieces for i, m in enumerate(ms)}
    return jnp.concatenate([found[m] for m in range(len(found))])


def two_terms(low):
    high = lax.reduce_precision(low, 8, 7)
    return jnp.concatenate([high, low - high], axis=-1).astype(jnp.bfloat16)


def one_term(sent):
    sent = sent.astype(jnp.float32)
    return sent[..., :RANK] + sent[..., RANK:]


def adapter_columns(adapter):
    return pl.ds(pl.multiple_of((adapter // 2) * PAIR, PAIR), PAIR)


def adapter_half(both, adapter):
    return jnp.where(adapter % 2 == 0, both[:, :RANK], both[:, RANK:])


def on_diagonal(update):
    row = lax.broadcasted_iota(jnp.int32, update.shape, 0) // BLK
    column = lax.broadcasted_iota(jnp.int32, update.shape, 1) // RANK
    return jnp.where(row == column, update, jnp.zeros_like(update))


def grouped(refs, counts):
    refs = iter(refs)
    return [[next(refs) for _ in range(n)] for n in counts]


def whole(parts):
    return parts[0][...] if len(parts) == 1 else jnp.concatenate([p[...] for p in parts], axis=0)


def flat(slots):
    return [part for parts in slots for part in parts]


def call(kernel, out_shape, scalars, arrays, limit=60, scratch=()):
    vmem, smem = pl.BlockSpec(memory_space=pltpu.VMEM), pl.BlockSpec(memory_space=pltpu.SMEM)
    return pl.pallas_call(
        kernel,
        out_shape=out_shape,
        in_specs=[smem] * len(scalars) + [vmem] * len(arrays),
        out_specs=jax.tree.map(lambda _: vmem, out_shape),
        scratch_shapes=scratch,
        cost_estimate=QUICK,
        compiler_params=pltpu.CompilerParams(vmem_limit_bytes=limit * MIB),
    )(*scalars, *arrays)


def first_kernel(counts, wanted, line_ref, tenant_ref, tokens_ref, gain_ref, up_ref, table_ref, inverse_ref, *refs):
    slots = len(counts)
    for d, devices_blocks in enumerate(wanted):
        write_columns([tenant_ref[b] for b in devices_blocks], up_ref, table_ref.at[d])
    features = tokens_ref.shape[1]
    width = features // slots
    total = jnp.zeros(inverse_ref.shape, jnp.float32)
    for s in range(slots):
        wide = tokens_ref[:, s * width : (s + 1) * width].astype(jnp.float32)
        total += jnp.sum(wide * wide, axis=1, keepdims=True)
    inverse = lax.rsqrt(total / features + norm_eps)
    inverse_ref[...] = inverse
    for s in range(slots):
        columns = pl.ds(pl.multiple_of((line_ref[0] ^ s) * width, width), width)
        wide = tokens_ref[:, columns].astype(jnp.float32)
        normed = (wide * inverse * gain_ref[:, columns]).astype(jnp.bfloat16)
        for part, ref in enumerate(grouped(refs, counts)[s]):
            ref[...] = normed[part * ref.shape[0] : (part + 1) * ref.shape[0]]


def parted(counts, rows, width):
    return [jax.ShapeDtypeStruct((rows // n, width), jnp.bfloat16) for n in counts for _ in range(n)]


def norm_and_up(line, tenant, tokens, gain, up_factor, counts, wanted):
    rows, features = tokens.shape
    shapes = [
        jax.ShapeDtypeStruct((len(wanted), up_factor.shape[0], len(wanted[0]) * RANK), up_factor.dtype),
        jax.ShapeDtypeStruct((rows, 1), jnp.float32),
    ] + parted(counts, rows, features // len(counts))
    table, inverse, *normed = call(
        functools.partial(first_kernel, counts, wanted), shapes, [line, tenant], [tokens, gain, up_factor]
    )
    return table, inverse, grouped(normed, counts)


def write_columns(adapters, factor_ref, out_ref):
    for first in range(0, len(adapters), 2):
        parts = [adapter_half(factor_ref[:, adapter_columns(a)], a) for a in adapters[first : first + 2]]
        out_ref[:, first * RANK : first * RANK + PAIR] = jnp.concatenate(parts, axis=1)


def class_adapters(place_ref, tenant_ref, size, blocks, r):
    devices = [(place_ref[0] ^ s) * 4 + (place_ref[1] ^ r) for s in range(size)]
    return [tenant_ref[d * blocks + b] for d in devices for b in range(blocks)]


def down_kernel(size, blocks, place_ref, tenant_ref, factor_ref, mine_ref, core_ref, pair_ref):
    for r, ref in enumerate((mine_ref, core_ref, pair_ref.at[0], pair_ref.at[1])):
        write_columns(class_adapters(place_ref, tenant_ref, size, blocks, r), factor_ref, ref)


def down_columns(place, tenant, down_factor, size, blocks):
    shape = (down_factor.shape[0], size * blocks * RANK)
    shapes = [jax.ShapeDtypeStruct(lead + shape, down_factor.dtype) for lead in ((), (), (2,))]
    return call(functools.partial(down_kernel, size, blocks), shapes, [place, tenant], [down_factor])


def scaled_kernel(upstream_ref, far_ref, up_ref, out_ref):
    rows = upstream_ref.shape[0]
    for which, ref in enumerate((upstream_ref, far_ref)):
        mixed = jnp.dot(ref[...], up_ref[...], preferred_element_type=jnp.float32)
        for b in range(rows // BLK):
            at = which * rows + b * BLK
            block = mixed[b * BLK : (b + 1) * BLK, at // BLK * RANK : (at // BLK + 1) * RANK]
            scaled = (adapter_scale * block).astype(out_ref.dtype)
            out_ref[at : at + BLK, :] = jnp.concatenate([scaled, scaled], axis=1)


def back_kernel(pieces, counts, rows, weight_ref, down_ref, scaled_ref, *refs):
    upstream_refs, out_refs = refs[: len(pieces)], grouped(refs[len(pieces) :], counts)
    contract = (((1,), (1,)), ((), ()))
    for upstream_ref, slots in zip(upstream_refs, pieces):
        product = lax.dot_general(
            upstream_ref[...], weight_ref[...], contract, preferred_element_type=jnp.float32
        )
        for at, slot in enumerate(slots):
            for r in range(0, rows, 2 * BLK):
                first, held = at * rows + r, slot * rows + r
                column = held // BLK * RANK
                term = lax.dot_general(
                    on_diagonal(scaled_ref[held : held + 2 * BLK, :]),
                    down_ref[:, column : column + PAIR],
                    contract,
                    preferred_element_type=jnp.float32,
                )
                back = (product[first : first + 2 * BLK] + term).astype(jnp.bfloat16)
                part = rows // counts[slot]
                step = min(part, 2 * BLK)
                for at_row in range(r, r + 2 * BLK, step):
                    inside = at_row % part
                    out_refs[slot][at_row // part][inside : inside + step, :] = back[at_row - r : at_row - r + step]


def value_kernel(counts, weight_ref, down_ref, *refs):
    normed_refs, (values_ref, low_ref, sent_ref) = grouped(refs[:-3], counts), refs[-3:]
    value_width = weight_ref.shape[1]
    for slot, parts in enumerate(normed_refs):
        normed = whole(parts)
        rows = normed.shape[0]
        values = jnp.dot(normed, weight_ref[...], preferred_element_type=jnp.float32)
        low = []
        for b in range(rows // BLK):
            column = (slot * rows // BLK + b) // 2 * PAIR
            both = jnp.dot(
                normed[b * BLK : (b + 1) * BLK],
                down_ref[:, column : column + PAIR],
                preferred_element_type=jnp.float32,
            )
            low.append(both[:, b % 2 * RANK : (b % 2 + 1) * RANK])
        low = jnp.concatenate(low, axis=0)
        if slot % 2:
            high = low.astype(jnp.bfloat16)
            rest = (low - high.astype(jnp.float32)).astype(jnp.bfloat16)
            sent_ref[slot // 2, :, :value_width] = values.astype(jnp.bfloat16)
            sent_ref[slot // 2, :, value_width:] = jnp.concatenate([high, rest], axis=1)
        else:
            values_ref[slot // 2] = values
            low_ref[slot // 2] = low


def value_products(weight, down, normed):
    rows, half, value_width = normed[0][0].shape[0], len(normed) // 2, weight.shape[1]
    shapes = [
        jax.ShapeDtypeStruct((half, rows, value_width), jnp.float32),
        jax.ShapeDtypeStruct((half, rows, RANK), jnp.float32),
        jax.ShapeDtypeStruct((half, rows, value_width + PAIR), jnp.bfloat16),
    ]
    counts = [len(parts) for parts in normed]
    return call(functools.partial(value_kernel, counts), shapes, [], [weight, down, *flat(normed)])


def sum_over_line(values, low, crossed, meanwhile):
    value_width, far, step = values.shape[-1], lax.axis_size("line") // 2, 2
    values = values + crossed[..., :value_width].astype(jnp.float32)
    low = low + one_term(crossed[..., value_width:])
    while step < far:
        low = low[::2] + one_term(over_line(two_terms(low[1::2]), step))
        values = values[::2] + over_line(values[1::2].astype(jnp.bfloat16), step).astype(jnp.float32)
        step *= 2
    return values, low + one_term(after(over_line(two_terms(low), far), meanwhile))[::-1]


def terms_kernel(counts, scale, place_ref, update_ref, *refs):
    rows_refs, (mine_ref, core_ref, pair_ref, scratch) = grouped(refs[:-4], counts), refs[-4:]
    rows, width = rows_refs[0][0].shape
    shard = width // 4
    for slot, parts in enumerate(rows_refs):
        held = whole(parts)
        for r in range(0, rows, 2 * BLK):
            first = slot * rows + r
            term = scale * lax.dot_general(
                held[r : r + 2 * BLK, :],
                on_diagonal(update_ref[first : first + 2 * BLK, :]),
                (((0,), (0,)), ((), ())),
                preferred_element_type=jnp.float32,
            )
            for p in range(4):
                scratch[p] = term[p * shard : (p + 1) * shard]
            columns = slice(first // BLK * RANK, first // BLK * RANK + PAIR)
            for r4, ref in enumerate((mine_ref, core_ref, pair_ref.at[0], pair_ref.at[1])):
                ref[:, columns] = scratch[place_ref[1] ^ r4].astype(jnp.bfloat16)


def factor_terms(place, update, rows, scale):
    count, width = rows[0][0].shape
    shape = (width // 4, len(rows) * count // BLK * RANK)
    counts = [len(parts) for parts in rows]
    return call(
        functools.partial(terms_kernel, counts, scale),
        [jax.ShapeDtypeStruct(lead + shape, jnp.bfloat16) for lead in ((), (), (2,))],
        [place],
        [update, *flat(rows)],
        scratch=[pltpu.VMEM((4, width // 4, PAIR), jnp.float32)],
    )


def owner_kernel(size, blocks, place_ref, tenant_ref, *refs):
    out_ref = refs[-1]
    out_ref[...] = jnp.zeros_like(out_ref)
    lane = lax.broadcasted_iota(jnp.int32, (out_ref.shape[0], PAIR), 1) // RANK
    for r, terms_ref in enumerate(refs[:-1]):
        adapters = class_adapters(place_ref, tenant_ref, size, blocks, r)
        for first in range(0, len(adapters), 2):
            columns = slice(first * RANK, first * RANK + PAIR)
            both = terms_ref[:, columns] if len(terms_ref.shape) == 2 else terms_ref[0, :, columns]
            both = both.astype(jnp.float32)
            turned = jnp.concatenate([both[:, RANK:], both[:, :RANK]], axis=1)
            for h, adapter in enumerate(adapters[first : first + 2]):
                side = adapter % 2
                term = jnp.where(side == h, both, turned)
                out_ref[:, adapter_columns(adapter)] += jnp.where(lane == side, term, jnp.zeros_like(term))


def owner_sums(place, tenant, size, terms, width):
    blocks = terms[0].shape[1] // RANK // size
    shape = jax.ShapeDtypeStruct((terms[0].shape[0], width), jnp.float32)
    return call(functools.partial(owner_kernel, size, blocks), shape, [place, tenant], terms)


def token_grad_kernel(counts, line_ref, tokens_ref, gain_ref, inverse_ref, *refs):
    back_refs, out_ref = grouped(refs[:-1], counts), refs[-1]
    slots, width = len(counts), back_refs[0][0].shape[1]
    inverse = inverse_ref[...]
    total = jnp.zeros_like(inverse)

    def load(s):
        columns = pl.ds(pl.multiple_of((line_ref[0] ^ s) * width, width), width)
        gained = gain_ref[:, columns] * whole(back_refs[s]).astype(jnp.float32)
        return columns, gained, tokens_ref[:, columns].astype(jnp.float32)

    for s in range(slots):
        _, gained, wide = load(s)
        total += jnp.sum(gained * wide, axis=1, keepdims=True)
    cubed = inverse * inverse * inverse
    inner = total / tokens_ref.shape[1]
    for s in range(slots):
        columns, gained, wide = load(s)
        out_ref[:, columns] = (inverse * gained - wide * cubed * inner).astype(out_ref.dtype)


def on_device(tokens, upstream, norm_gain, value_weight, down_factor, up_factor, tenant):
    size, far = lax.axis_size("line"), lax.axis_size("line") // 2
    line, pair, core = lax.axis_index("line"), lax.axis_index("pair"), lax.axis_index("core")
    place = 2 * pair + core
    line_, place_ = line.reshape(1), jnp.stack([line, place])
    rows = tokens.shape[0]
    blocks = rows // BLK
    value_width = upstream.shape[1]
    adapter_width = down_factor.shape[1]
    value_rows = up_factor.shape[0]
    gain = norm_gain.reshape(1, -1)

    upstream_far = over_line(upstream, far)

    wanted = [
        [e * blocks + b for e in (d, d ^ (4 * far)) for b in range(blocks)] for d in range(4 * size)
    ]
    counts = [1] * size
    up_sent, inverse, normed = norm_and_up(line_, tenant, tokens, gain, up_factor, counts, wanted)
    crossed_far = over_line(after(normed[far][0], upstream_far), far)

    up_mine = lax.all_to_all(
        after(up_sent, upstream_far, over_cores(inverse)), ("line", "pair", "core"), split_axis=0, concat_axis=0, tiled=True
    )
    up_mine = up_mine.reshape(value_width, 2 * blocks * RANK)

    pieces = gather_line(jnp.concatenate([upstream, upstream_far]))
    across = over_pair(value_weight)
    down_mine, down_core, down_pair = down_columns(
        place_, tenant, after(down_factor, normed[0][0]), size, blocks
    )
    down_crossed = over_pair(down_pair)

    scaled = call(
        scaled_kernel,
        jax.ShapeDtypeStruct((2 * rows, PAIR), jnp.bfloat16),
        [],
        [after(upstream, crossed_far, across, down_crossed, *[p for p, _ in pieces]), upstream_far, up_mine],
    )
    across, down_crossed, down_core, weight_mine, scaled = lax.optimization_barrier(
        (across, down_crossed, down_core, value_weight, scaled)
    )
    weight = in_order([weight_mine, over_cores(weight_mine), across, over_cores(across)], place)
    down = in_order([down_mine, over_cores(down_core), down_crossed, over_cores(down_crossed[1])], place)
    scaled = in_slots(gather_line(scaled))
    arrived = [normed[0]] + [[over_line(after(normed[s][0], scaled), s)] for s in range(1, size)]
    arrived[far] = [crossed_far]

    counts = [1] * far + [2] + [1] * (far - 1)
    back = call(
        functools.partial(back_kernel, [s for _, s in pieces], counts, rows),
        parted(counts, rows, weight.shape[0]),
        [],
        [weight, down, scaled] + [p for p, _ in pieces],
    )
    back = grouped(back, counts)
    first = over_line(back[far][0], far)

    terms = factor_terms(place_, after(scaled, back[0][0]), arrived, 1.0)
    values, low, sent = value_products(after(weight, terms[0]), down, arrived)
    back_mine = [back[0]] + [[over_line(back[s][0], s)] for s in range(1, far)]
    crossed = over_line(after(sent, first, *flat(back_mine)), 1)
    back_mine += [[first, over_line(after(back[far][1], first), far)]]

    crossed_terms = over_pair(terms[2])
    terms = [terms[0], over_cores(terms[1]), crossed_terms, over_cores(crossed_terms[1])]
    grad_down = owner_sums(place_, tenant, size, terms, adapter_width)

    values, low = sum_over_line(values, low, crossed, grad_down)
    low = low.astype(jnp.bfloat16)
    back_mine += [[over_line(after(back[s][0], crossed), s)] for s in range(far + 1, size)]
    last = over_line(after(values[1].astype(jnp.bfloat16), low), far)
    values = values[0] + last.astype(jnp.float32)
    columns = [
        (lax.dynamic_slice_in_dim(p, line * 4 * value_rows, 4 * value_rows, 1), s)
        for p, s in pieces
    ]
    low_held = jnp.concatenate([low, low], axis=-1).reshape(2 * rows, PAIR)
    low_all = after(in_slots(gather_line(low_held)), *flat(back_mine[far + 1 :]))
    terms = factor_terms(place_, low_all, [[in_slots(columns)]], adapter_scale)
    crossed_terms = over_pair(terms[2])
    grad_tokens = call(
        functools.partial(token_grad_kernel, counts),
        jax.ShapeDtypeStruct(tokens.shape, tokens.dtype),
        [line_],
        [tokens, gain, after(inverse, terms[0]), *flat(back_mine)],
        32,
    )
    crossed_terms = after(crossed_terms, grad_tokens, last)
    terms = [terms[0], over_cores(terms[1]), crossed_terms, over_cores(crossed_terms[1])]
    grad_up = owner_sums(place_, tenant, size, terms, adapter_width)

    adapter_branch = jnp.einsum(
        "bkr,vbr->bkv",
        low[0].reshape(blocks, BLK, RANK),
        up_mine[:, : blocks * RANK].reshape(value_width, blocks, RANK),
        preferred_element_type=jnp.float32,
    ).reshape(rows, value_width)
    adapted_values = (values + adapter_scale * adapter_branch).astype(jnp.bfloat16)

    return (adapted_values, grad_tokens, grad_down, grad_up)


def solution(mesh):
    groups, shards = mesh.shape["groups"], mesh.shape["fsdp"]
    line_mesh = Mesh(mesh.devices.reshape(groups, shards // 4, 2, 2), ("groups", "line", "pair", "core"))
    own = ("line", "pair", "core")
    everywhere = P(("groups",) + own, None)
    in_specs = (everywhere, everywhere, P(), P(own, None), P(own, None), P(own, None), P("groups"))
    out_specs = (everywhere,) * 4
    return jax.shard_map(
        on_device, mesh=line_mesh, in_specs=in_specs, out_specs=out_specs, check_vma=False
    )
```

```python
import functools

import jax
import jax.numpy as jnp
from jax import lax
from jax.experimental import pallas as pl
from jax.experimental.pallas import tpu as pltpu
from jax.sharding import Mesh
from jax.sharding import PartitionSpec as P

RANK = 64
BLK = 64
PAIR = 2 * RANK

adapter_scale = 0.5
norm_eps = 1e-05

QUICK = pl.CostEstimate(flops=1, bytes_accessed=1, transcendentals=0)
MIB = 1024 * 1024


def over_line(value, mask):
    size = lax.axis_size("line")
    return lax.ppermute(value, "line", [(i, i ^ mask) for i in range(size)])


def over_pair(value):
    return lax.ppermute(value, "pair", [(0, 1), (1, 0)])


def over_cores(value):
    return lax.ppermute(value, "core", [(0, 1), (1, 0)])


def after(value, *others):
    return lax.optimization_barrier((value,) + others)[0]


def order_kernel(place_ref, mine_ref, beside_ref, across_ref, corner_ref, out_ref):
    for r, ref in enumerate((mine_ref, beside_ref, across_ref, corner_ref)):
        out_ref[place_ref[0] ^ r] = ref[...] if len(ref.shape) == 2 else ref[0]


def in_order(parts, place):
    rows, width = parts[0].shape
    shape = jax.ShapeDtypeStruct((4, rows, width), parts[0].dtype)
    return call(order_kernel, shape, [place.reshape(1)], parts, 20).reshape(4 * rows, width)


def gather_line(held):
    size = lax.axis_size("line")
    pieces, slots, step = [(held, [0, size // 2])], [0, size // 2], size // 4
    while step:
        arrived = over_line(held, step)
        more = [s ^ step for s in slots]
        pieces.append((arrived, more))
        slots, step = slots + more, step // 2
        held = jnp.concatenate([held, arrived]) if step else held
    return pieces


def in_slots(pieces):
    rows = pieces[0][0].shape[0] // 2
    found = {m: p[i * rows : (i + 1) * rows] for p, ms in pieces for i, m in enumerate(ms)}
    return jnp.concatenate([found[m] for m in range(len(found))])


def two_terms(low):
    high = lax.reduce_precision(low, 8, 7)
    return jnp.concatenate([high, low - high], axis=-1).astype(jnp.bfloat16)


def one_term(sent):
    sent = sent.astype(jnp.float32)
    return sent[..., :RANK] + sent[..., RANK:]


def adapter_columns(adapter):
    return pl.ds(pl.multiple_of((adapter // 2) * PAIR, PAIR), PAIR)


def adapter_half(both, adapter):
    return jnp.where(adapter % 2 == 0, both[:, :RANK], both[:, RANK:])


def on_diagonal(update):
    row = lax.broadcasted_iota(jnp.int32, update.shape, 0) // BLK
    column = lax.broadcasted_iota(jnp.int32, update.shape, 1) // RANK
    return jnp.where(row == column, update, jnp.zeros_like(update))


def grouped(refs, counts):
    refs = iter(refs)
    return [[next(refs) for _ in range(n)] for n in counts]


def whole(parts):
    return parts[0][...] if len(parts) == 1 else jnp.concatenate([p[...] for p in parts], axis=0)


def flat(slots):
    return [part for parts in slots for part in parts]


def call(kernel, out_shape, scalars, arrays, limit=60, scratch=()):
    vmem, smem = pl.BlockSpec(memory_space=pltpu.VMEM), pl.BlockSpec(memory_space=pltpu.SMEM)
    return pl.pallas_call(
        kernel,
        out_shape=out_shape,
        in_specs=[smem] * len(scalars) + [vmem] * len(arrays),
        out_specs=jax.tree.map(lambda _: vmem, out_shape),
        scratch_shapes=scratch,
        cost_estimate=QUICK,
        compiler_params=pltpu.CompilerParams(vmem_limit_bytes=limit * MIB),
    )(*scalars, *arrays)


def first_kernel(counts, wanted, line_ref, tenant_ref, tokens_ref, gain_ref, up_ref, table_ref, inverse_ref, *refs):
    slots = len(counts)
    for d, devices_blocks in enumerate(wanted):
        write_columns([tenant_ref[b] for b in devices_blocks], up_ref, table_ref.at[d])
    features = tokens_ref.shape[1]
    width = features // slots
    total = jnp.zeros(inverse_ref.shape, jnp.float32)
    for s in range(slots):
        wide = tokens_ref[:, s * width : (s + 1) * width].astype(jnp.float32)
        total += jnp.sum(wide * wide, axis=1, keepdims=True)
    inverse = lax.rsqrt(total / features + norm_eps)
    inverse_ref[...] = inverse
    for s in range(slots):
        columns = pl.ds(pl.multiple_of((line_ref[0] ^ s) * width, width), width)
        wide = tokens_ref[:, columns].astype(jnp.float32)
        normed = (wide * inverse * gain_ref[:, columns]).astype(jnp.bfloat16)
        for part, ref in enumerate(grouped(refs, counts)[s]):
            ref[...] = normed[part * ref.shape[0] : (part + 1) * ref.shape[0]]


def parted(counts, rows, width):
    return [jax.ShapeDtypeStruct((rows // n, width), jnp.bfloat16) for n in counts for _ in range(n)]


def norm_and_up(line, tenant, tokens, gain, up_factor, counts, wanted):
    rows, features = tokens.shape
    shapes = [
        jax.ShapeDtypeStruct((len(wanted), up_factor.shape[0], len(wanted[0]) * RANK), up_factor.dtype),
        jax.ShapeDtypeStruct((rows, 1), jnp.float32),
    ] + parted(counts, rows, features // len(counts))
    table, inverse, *normed = call(
        functools.partial(first_kernel, counts, wanted), shapes, [line, tenant], [tokens, gain, up_factor]
    )
    return table, inverse, grouped(normed, counts)


def write_columns(adapters, factor_ref, out_ref):
    for first in range(0, len(adapters), 2):
        parts = [adapter_half(factor_ref[:, adapter_columns(a)], a) for a in adapters[first : first + 2]]
        out_ref[:, first * RANK : first * RANK + PAIR] = jnp.concatenate(parts, axis=1)


def class_adapters(place_ref, tenant_ref, slots, blocks, r):
    devices = [(place_ref[0] ^ s) * 4 + (place_ref[1] ^ r) for s in slots]
    return [tenant_ref[d * blocks + b] for d in devices for b in range(blocks)]


def down_kernel(size, blocks, place_ref, tenant_ref, factor_ref, mine_ref, core_ref, pair_ref):
    for r, ref in enumerate((mine_ref, core_ref, pair_ref.at[0], pair_ref.at[1])):
        write_columns(class_adapters(place_ref, tenant_ref, range(size), blocks, r), factor_ref, ref)


def down_columns(place, tenant, down_factor, size, blocks):
    shape = (down_factor.shape[0], size * blocks * RANK)
    shapes = [jax.ShapeDtypeStruct(lead + shape, down_factor.dtype) for lead in ((), (), (2,))]
    return call(functools.partial(down_kernel, size, blocks), shapes, [place, tenant], [down_factor])


def scaled_kernel(upstream_ref, far_ref, up_ref, out_ref):
    rows = upstream_ref.shape[0]
    for which, ref in enumerate((upstream_ref, far_ref)):
        mixed = jnp.dot(ref[...], up_ref[...], preferred_element_type=jnp.float32)
        for b in range(rows // BLK):
            at = which * rows + b * BLK
            block = mixed[b * BLK : (b + 1) * BLK, at // BLK * RANK : (at // BLK + 1) * RANK]
            scaled = (adapter_scale * block).astype(out_ref.dtype)
            out_ref[at : at + BLK, :] = jnp.concatenate([scaled, scaled], axis=1)


def back_kernel(pieces, counts, rows, weight_ref, down_ref, scaled_ref, *refs):
    upstream_refs, out_refs = refs[: len(pieces)], grouped(refs[len(pieces) :], counts)
    contract = (((1,), (1,)), ((), ()))
    for upstream_ref, slots in zip(upstream_refs, pieces):
        product = lax.dot_general(
            upstream_ref[...], weight_ref[...], contract, preferred_element_type=jnp.float32
        )
        for at, slot in enumerate(slots):
            for r in range(0, rows, 2 * BLK):
                first, held = at * rows + r, slot * rows + r
                column = held // BLK * RANK
                term = lax.dot_general(
                    on_diagonal(scaled_ref[held : held + 2 * BLK, :]),
                    down_ref[:, column : column + PAIR],
                    contract,
                    preferred_element_type=jnp.float32,
                )
                back = (product[first : first + 2 * BLK] + term).astype(jnp.bfloat16)
                part = rows // counts[slot]
                step = min(part, 2 * BLK)
                for at_row in range(r, r + 2 * BLK, step):
                    inside = at_row % part
                    out_refs[slot][at_row // part][inside : inside + step, :] = back[at_row - r : at_row - r + step]


def value_kernel(counts, weight_ref, down_ref, *refs):
    normed_refs, (values_ref, low_ref, sent_ref) = grouped(refs[:-3], counts), refs[-3:]
    value_width = weight_ref.shape[1]
    for slot, parts in enumerate(normed_refs):
        normed = whole(parts)
        rows = normed.shape[0]
        values = jnp.dot(normed, weight_ref[...], preferred_element_type=jnp.float32)
        low = []
        for b in range(rows // BLK):
            column = (slot * rows // BLK + b) // 2 * PAIR
            both = jnp.dot(
                normed[b * BLK : (b + 1) * BLK],
                down_ref[:, column : column + PAIR],
                preferred_element_type=jnp.float32,
            )
            low.append(both[:, b % 2 * RANK : (b % 2 + 1) * RANK])
        low = jnp.concatenate(low, axis=0)
        if slot % 2:
            high = low.astype(jnp.bfloat16)
            rest = (low - high.astype(jnp.float32)).astype(jnp.bfloat16)
            sent_ref[slot // 2, :, :value_width] = values.astype(jnp.bfloat16)
            sent_ref[slot // 2, :, value_width:] = jnp.concatenate([high, rest], axis=1)
        else:
            values_ref[slot // 2] = values
            low_ref[slot // 2] = low


def value_products(weight, down, normed):
    rows, half, value_width = normed[0][0].shape[0], len(normed) // 2, weight.shape[1]
    shapes = [
        jax.ShapeDtypeStruct((half, rows, value_width), jnp.float32),
        jax.ShapeDtypeStruct((half, rows, RANK), jnp.float32),
        jax.ShapeDtypeStruct((half, rows, value_width + PAIR), jnp.bfloat16),
    ]
    counts = [len(parts) for parts in normed]
    return call(functools.partial(value_kernel, counts), shapes, [], [weight, down, *flat(normed)], 32)


def sum_over_line(values, low, crossed):
    value_width, far, step = values.shape[-1], lax.axis_size("line") // 2, 2
    values = values + crossed[..., :value_width].astype(jnp.float32)
    low = low + one_term(crossed[..., value_width:])
    while step < far:
        low = low[::2] + one_term(over_line(two_terms(low[1::2]), step))
        values = values[::2] + over_line(values[1::2].astype(jnp.bfloat16), step).astype(jnp.float32)
        step *= 2
    return values, low + one_term(over_line(two_terms(low), far))[::-1]


def terms_kernel(counts, slots, scale, place_ref, update_ref, *refs):
    rows_refs, (mine_ref, core_ref, pair_ref, scratch) = grouped(refs[:-4], counts), refs[-4:]
    rows, width = rows_refs[0][0].shape
    shard = width // 4
    for at, (slot, parts) in enumerate(zip(slots, rows_refs)):
        held = whole(parts)
        for r in range(0, rows, 2 * BLK):
            first, column = slot * rows + r, (at * rows + r) // BLK * RANK
            term = scale * lax.dot_general(
                held[r : r + 2 * BLK, :],
                on_diagonal(update_ref[first : first + 2 * BLK, :]),
                (((0,), (0,)), ((), ())),
                preferred_element_type=jnp.float32,
            )
            for p in range(4):
                scratch[p] = term[p * shard : (p + 1) * shard]
            columns = slice(column, column + PAIR)
            for r4, ref in enumerate((mine_ref, core_ref, pair_ref.at[0], pair_ref.at[1])):
                ref[:, columns] = scratch[place_ref[1] ^ r4].astype(jnp.bfloat16)


def factor_terms(place, update, rows, slots, scale):
    count, width = rows[0][0].shape[0], rows[0][0].shape[1]
    shape = (width // 4, len(rows) * count // BLK * RANK)
    counts = [len(parts) for parts in rows]
    return call(
        functools.partial(terms_kernel, counts, slots, scale),
        [jax.ShapeDtypeStruct(lead + shape, jnp.bfloat16) for lead in ((), (), (2,))],
        [place],
        [update, *flat(rows)],
        32,
        scratch=[pltpu.VMEM((4, width // 4, PAIR), jnp.float32)],
    )


def owner_kernel(groups, blocks, place_ref, tenant_ref, *refs):
    out_ref = refs[-1]
    out_ref[...] = jnp.zeros_like(out_ref)
    lane = lax.broadcasted_iota(jnp.int32, (out_ref.shape[0], PAIR), 1) // RANK
    for at, terms_ref in enumerate(refs[:-1]):
        adapters = class_adapters(place_ref, tenant_ref, groups[at // 4], blocks, at % 4)
        for first in range(0, len(adapters), 2):
            columns = slice(first * RANK, first * RANK + PAIR)
            both = terms_ref[:, columns] if len(terms_ref.shape) == 2 else terms_ref[0, :, columns]
            both = both.astype(jnp.float32)
            turned = jnp.concatenate([both[:, RANK:], both[:, :RANK]], axis=1)
            for h, adapter in enumerate(adapters[first : first + 2]):
                side = adapter % 2
                term = jnp.where(side == h, both, turned)
                out_ref[:, adapter_columns(adapter)] += jnp.where(lane == side, term, jnp.zeros_like(term))


def owner_sums(place, tenant, groups, terms, width):
    blocks = terms[0].shape[1] // RANK // len(groups[0])
    shape = jax.ShapeDtypeStruct((terms[0].shape[0], width), jnp.float32)
    return call(functools.partial(owner_kernel, groups, blocks), shape, [place, tenant], terms, 24)


def four_terms(terms, crossed):
    return [terms[0], over_cores(terms[1]), crossed, over_cores(crossed[1])]


def token_grad_kernel(counts, line_ref, tokens_ref, gain_ref, inverse_ref, *refs):
    back_refs, out_ref = grouped(refs[:-1], counts), refs[-1]
    slots, width = len(counts), back_refs[0][0].shape[1]
    inverse = inverse_ref[...]
    total = jnp.zeros_like(inverse)

    def load(s):
        columns = pl.ds(pl.multiple_of((line_ref[0] ^ s) * width, width), width)
        gained = gain_ref[:, columns] * whole(back_refs[s]).astype(jnp.float32)
        return columns, gained, tokens_ref[:, columns].astype(jnp.float32)

    for s in range(slots):
        _, gained, wide = load(s)
        total += jnp.sum(gained * wide, axis=1, keepdims=True)
    cubed = inverse * inverse * inverse
    inner = total / tokens_ref.shape[1]
    for s in range(slots):
        columns, gained, wide = load(s)
        out_ref[:, columns] = (inverse * gained - wide * cubed * inner).astype(out_ref.dtype)


def on_device(tokens, upstream, norm_gain, value_weight, down_factor, up_factor, tenant):
    size, far = lax.axis_size("line"), lax.axis_size("line") // 2
    line, pair, core = lax.axis_index("line"), lax.axis_index("pair"), lax.axis_index("core")
    place = 2 * pair + core
    line_, place_ = line.reshape(1), jnp.stack([line, place])
    rows = tokens.shape[0]
    blocks = rows // BLK
    value_width = upstream.shape[1]
    adapter_width = down_factor.shape[1]
    value_rows = up_factor.shape[0]
    gain = norm_gain.reshape(1, -1)

    upstream_far = over_line(upstream, far)

    wanted = [
        [e * blocks + b for e in (d, d ^ (4 * far)) for b in range(blocks)] for d in range(4 * size)
    ]
    counts = [1] * size
    up_sent, inverse, normed = norm_and_up(line_, tenant, tokens, gain, up_factor, counts, wanted)
    crossed_far = over_line(after(normed[far][0], upstream_far), far)

    up_mine = lax.all_to_all(
        after(up_sent, upstream_far, over_cores(inverse)), ("line", "pair", "core"), split_axis=0, concat_axis=0, tiled=True
    )
    up_mine = up_mine.reshape(value_width, 2 * blocks * RANK)

    pieces = gather_line(jnp.concatenate([upstream, upstream_far]))
    across = over_pair(value_weight)
    down_mine, down_core, down_pair = down_columns(
        place_, tenant, after(down_factor, normed[0][0]), size, blocks
    )
    down_crossed = over_pair(down_pair)

    scaled = call(
        scaled_kernel,
        jax.ShapeDtypeStruct((2 * rows, PAIR), jnp.bfloat16),
        [],
        [after(upstream, crossed_far, across, down_crossed, *[p for p, _ in pieces]), upstream_far, up_mine],
    )
    across, down_crossed, down_core, weight_mine, scaled = lax.optimization_barrier(
        (across, down_crossed, down_core, value_weight, scaled)
    )
    weight = in_order([weight_mine, over_cores(weight_mine), across, over_cores(across)], place)
    down = in_order([down_mine, over_cores(down_core), down_crossed, over_cores(down_crossed[1])], place)
    scaled = in_slots(gather_line(scaled))
    arrived = [normed[0]] + [[over_line(after(normed[s][0], scaled), s)] for s in range(1, size)]
    arrived[far] = [crossed_far]

    columns = [
        (lax.dynamic_slice_in_dim(p, line * 4 * value_rows, 4 * value_rows, 1), s)
        for p, s in pieces
    ]
    columns = in_slots(columns)

    early_slots, late_slots = [0, far], [s for s in range(1, size) if s != far]
    early = factor_terms(place_, scaled, [arrived[s] for s in early_slots], early_slots, 1.0)
    early_crossed = over_pair(early[2])

    counts = [1] * far + [2] + [1] * (far - 1)
    back = call(
        functools.partial(back_kernel, [s for _, s in pieces], counts, rows),
        parted(counts, rows, weight.shape[0]),
        [],
        [after(weight, early[0], columns), down, scaled] + [p for p, _ in pieces],
        32,
    )
    back = grouped(back, counts)
    first = over_line(back[far][0], far)

    values, low, sent = value_products(after(weight, back[0][0]), down, arrived)
    back_mine = [back[0]] + [[over_line(back[s][0], s)] for s in range(1, far)]
    crossed = over_line(after(sent, first, early_crossed, *flat(back_mine)), 1)
    back_mine += [[first, over_line(after(back[far][1], first), far)]]
    crossed = after(crossed, back_mine[far][1])

    late = factor_terms(place_, after(scaled, first, sent), [arrived[s] for s in late_slots], late_slots, 1.0)
    late_crossed = over_pair(late[2])
    early, late, early_crossed, late_crossed, _ = lax.optimization_barrier(
        (early[:2], late[:2], early_crossed, late_crossed, crossed)
    )
    terms = four_terms(early, early_crossed) + four_terms(late, late_crossed)
    grad_down = owner_sums(place_, tenant, [early_slots, late_slots], terms, adapter_width)

    values, low = sum_over_line(values, low, crossed)
    low = low.astype(jnp.bfloat16)
    back_mine += [[over_line(after(back[s][0], crossed), s)] for s in range(far + 1, size)]
    last = over_line(after(values[1].astype(jnp.bfloat16), *flat(back_mine[far + 1 :])), far)
    values = values[0] + last.astype(jnp.float32)
    low_held = jnp.concatenate([low, low], axis=-1).reshape(2 * rows, PAIR)
    low_pieces = [(after(p, grad_down), s) for p, s in gather_line(low_held)]
    low_all = after(in_slots(low_pieces), *flat(back_mine[far + 1 :]))
    terms = factor_terms(place_, low_all, [[columns]], [0], adapter_scale)
    crossed_terms = over_pair(terms[2])
    grad_tokens = call(
        functools.partial(token_grad_kernel, counts),
        jax.ShapeDtypeStruct(tokens.shape, tokens.dtype),
        [line_],
        [tokens, gain, after(inverse, terms[0]), *flat(back_mine)],
        32,
    )
    crossed_terms = after(crossed_terms, grad_tokens, last)
    terms = four_terms(terms, crossed_terms)
    grad_up = owner_sums(place_, tenant, [list(range(size))], terms, adapter_width)

    adapter_branch = jnp.einsum(
        "bkr,vbr->bkv",
        low[0].reshape(blocks, BLK, RANK),
        up_mine[:, : blocks * RANK].reshape(value_width, blocks, RANK),
        preferred_element_type=jnp.float32,
    ).reshape(rows, value_width)
    adapted_values = (values + adapter_scale * adapter_branch).astype(jnp.bfloat16)

    return (adapted_values, grad_tokens, grad_down, grad_up)


def solution(mesh):
    groups, shards = mesh.shape["groups"], mesh.shape["fsdp"]
    line_mesh = Mesh(mesh.devices.reshape(groups, shards // 4, 2, 2), ("groups", "line", "pair", "core"))
    own = ("line", "pair", "core")
    everywhere = P(("groups",) + own, None)
    in_specs = (everywhere, everywhere, P(), P(own, None), P(own, None), P(own, None), P("groups"))
    out_specs = (everywhere,) * 4
    return jax.shard_map(
        on_device, mesh=line_mesh, in_specs=in_specs, out_specs=out_specs, check_vma=False
    )
```
